32 devices in a mesh: lat: 16 (over z, x, core), lon: 2 (over y).
Axes of the slice: x: 2, y: 2, z: 4, core: 2. Of those that a mesh axis runs over, the one named last changes fastest.
Arguments:
- fields: bfloat16 [2, 16, 1024, 256], P(None, 'lat', 'lon'), may hold values from -6 to 6
- norm_gain: float32 [256], replicated, may hold values from 0.1 to 1.9
- w_qkv: bfloat16 [256, 768], replicated, may hold values from -12 to 12
- w_out: bfloat16 [256, 256], replicated, may hold values from -1 to 1
- conv_weight: bfloat16 [256, 4, 4, 128], replicated, may hold values from -0.1875 to 0.1875
- conv_bias: float32 [128], replicated, may hold values from -3 to 3
Outputs:
- upsampled: bfloat16 [2, 32, 2048, 128], P(None, 'lat', 'lon')
The draws below stay inside these ranges and needn't reach their ends.
All inputs are finite; a program needn't handle non-finite values.
Results may differ from the reference program's by a relative error of at most 0.0085.
Values may be sent and summed in bfloat16 or wider, within the bound.
A program may use at most 64 MiB of HBM per device.

```python
import math
import jax
import jax.numpy as jnp
from jax import lax

C = 256
HEADS = 8
CO = 128
B = 2
LAT = 16
LON = 1024


def common_pattern(key):
    pattern_key = jax.random.fold_in(key, 7)
    halves = (jax.random.randint(pattern_key, (C // 2,), 0, 2) * 2 - 1).astype(jnp.float32)
    paired = jnp.stack([halves, -halves], axis=1).reshape(C)
    return paired * C ** (-0.5)


def column_signs(key):
    sign_key = jax.random.fold_in(key, 13)
    return (jax.random.randint(sign_key, (C,), 0, 2) * 2 - 1).astype(jnp.float32)


def draw_fields(key, part):
    pattern = common_pattern(key)
    noise_key, column_key = jax.random.split(jax.random.fold_in(key, 11), 2)
    column = jax.random.randint(column_key, (B, LAT), 0, LON)
    noise = jnp.clip(jax.random.normal(noise_key, (B, LAT, LON, C), jnp.float32), -6.0, 6.0)
    share = 0.5
    marked = (jnp.arange(LON)[None, None, :] == column[..., None]).astype(jnp.float32)[..., None]
    scale = C ** 0.5
    drawn = share * scale * pattern + (1.0 - share * share) ** 0.5 * noise
    landmark = 0.95 * scale * pattern + 0.31 * noise
    result = marked * landmark + (1.0 - marked) * drawn
    return result.astype(jnp.bfloat16)


def draw_w_qkv(key, part):
    first_key = jax.random.fold_in(key, 0)
    factor = C ** (-0.5)
    base = jnp.clip(jax.random.normal(first_key, (C, 3 * C), jnp.float32), -6.0, 6.0) * factor
    pattern = common_pattern(key)
    step_scale = math.log(LON) / (C * 0.5 * 0.45)
    magnitude = (step_scale / (C // HEADS) ** 0.5) ** 0.5
    shared = pattern[:, None] * (magnitude * column_signs(key))[None, :]
    query_block = 0.3 * base[:, :C] + shared
    key_block = 0.3 * base[:, C:2 * C] + shared
    result = jnp.concatenate([query_block, key_block, base[:, 2 * C:]], axis=1)
    return result.astype(jnp.bfloat16)


def gaussian(rng, extent, spread, bound, dtype=jnp.bfloat16):
    return jnp.clip(spread * jax.random.normal(rng, extent, jnp.float32), -bound, bound).astype(dtype)


def setup_inputs(seed: int = 0) -> dict:
    seeds = jax.random.split(jax.random.key(seed), 7)
    return {
        "fields": draw_fields(jax.random.fold_in(seeds[6], 71), 0),
        "norm_gain": jnp.clip(1.0 + 0.18 * jax.random.normal(seeds[1], (C,), jnp.float32), 0.1, 1.9),
        "w_qkv": draw_w_qkv(jax.random.fold_in(seeds[6], 71), 0),
        "w_out": gaussian(seeds[3], (C, C), (C // 8) ** -0.5, 1.0),
        "conv_weight": gaussian(seeds[4], (C, 4, 4, CO), (4 * C) ** -0.5, 0.1875),
        "conv_bias": gaussian(seeds[5], (CO,), 0.5, 3.0, jnp.float32),
    }


def normalize(fields, norm_gain):
    values = fields.astype(jnp.float32)
    average = lax.optimization_barrier(jnp.mean(values, axis=-1, keepdims=True))
    centred = values - average
    variance = lax.optimization_barrier(jnp.mean(centred * centred, axis=-1, keepdims=True))
    return (centred * lax.rsqrt(variance + 1e-05) * norm_gain).astype(jnp.bfloat16)

def split_heads(row_block, head_count):
    seq_count, length, width = row_block.shape
    depth = width // head_count
    return row_block.reshape(seq_count, length, head_count, depth).transpose(0, 2, 1, 3).reshape(seq_count * head_count, length, depth)

def merge_heads(row_block, head_count):
    total_items, length, depth = row_block.shape
    seq_count = total_items // head_count
    return row_block.reshape(seq_count, head_count, length, depth).transpose(0, 2, 1, 3).reshape(seq_count, length, head_count * depth)

def attend_one(item_rows):
    query_one, key_one, value_one = item_rows
    scores = jnp.dot(query_one, key_one.T, preferred_element_type=jnp.float32) * query_one.shape[-1] ** (-0.5)
    maxima = lax.optimization_barrier(jnp.max(scores, axis=-1, keepdims=True))
    probs = jnp.exp(scores - maxima)
    totals = lax.optimization_barrier(jnp.sum(probs, axis=-1, keepdims=True))
    summed = jnp.dot(probs.astype(jnp.bfloat16), value_one, preferred_element_type=jnp.float32)
    return summed / totals

def attend_full(queries, keys_rows, values_rows, head_count):
    result = lax.map(attend_one, (split_heads(queries, head_count), split_heads(keys_rows, head_count), split_heads(values_rows, head_count)))
    return merge_heads(result, head_count).astype(jnp.bfloat16)

def upsample(sample, conv_weight, conv_bias):
    width = sample.shape[-1]
    outward = conv_weight.shape[-1]
    accum = jnp.zeros((LAT + 1, 2, LON + 1, 2, outward), jnp.float32)
    flat_rows = sample.reshape(-1, width)
    for row_tap in range(4):
        for col_tap in range(4):
            term = jnp.dot(flat_rows, conv_weight[:, row_tap, col_tap, :], preferred_element_type=jnp.float32).reshape(LAT, LON, outward)
            row_off = row_tap // 2
            col_off = col_tap // 2
            accum = accum.at[row_off:row_off + LAT, row_tap % 2, col_off:col_off + LON, col_tap % 2].add(term)
    tiled = accum.reshape(2 * LAT + 2, 2 * LON + 2, outward)
    middle = tiled[1:-1, 1:-1]
    middle = middle.at[:, 0].add(tiled[1:-1, -1]).at[:, -1].add(tiled[1:-1, 0])
    return (middle + conv_bias).astype(jnp.bfloat16)

def reference(fields, norm_gain, w_qkv, w_out, conv_weight, conv_bias):
    width = fields.shape[-1]
    normed = normalize(fields, norm_gain)
    flat_rows = normed.reshape(-1, width)
    projected = jnp.dot(flat_rows, w_qkv, preferred_element_type=jnp.float32).astype(jnp.bfloat16)
    projected = projected.reshape(B * LAT, LON, 3 * width)
    attended = attend_full(projected[..., :width], projected[..., width:2 * width], projected[..., 2 * width:], HEADS)
    update = jnp.dot(attended.reshape(-1, width), w_out, preferred_element_type=jnp.float32).reshape(fields.shape)
    hidden = (fields.astype(jnp.float32) + update).astype(jnp.bfloat16)
    return lax.map(lambda sample: upsample(sample, conv_weight, conv_bias), hidden)
```

```python
import functools
import math

import jax
import jax.numpy as jnp
from jax import lax
from jax.experimental import pallas as pl
from jax.experimental.pallas import tpu as pltpu
from jax.sharding import PartitionSpec as P

HEADS = 8
EDGE = 16
MESH = pl.DeviceIdType.MESH
F32 = jnp.float32
BF16 = jnp.bfloat16


def dot(a, b):
    return jnp.dot(a, b, preferred_element_type=F32)


def dot_nt(a, b):
    return lax.dot_general(a, b, (((1,), (1,)), ((), ())), preferred_element_type=F32)


def kernel(
    n_lat,
    n_lon,
    fields,
    gain,
    w_qkv,
    w_out,
    conv_w,
    bias,
    out,
    peers,
    queries,
    w_t,
    acc,
    maxima,
    att,
    hid,
    wide,
    f_send,
    f_recv,
    h_send,
    h_recv,
):
    batch, cols, width = fields.shape
    depth = width // HEADS
    outward = bias.shape[-1]
    lat = lax.axis_index("lat")
    lon = lax.axis_index("lon")
    scale = depth ** (-0.5) * math.log2(math.e)
    right = lax.rem(lon + 1, n_lon)
    left = lax.rem(lon + n_lon - 1, n_lon)
    has = {-1: lat > 0, 0: None, 1: lat < n_lat - 1}
    near = sorted({0, 1, n_lon - 1})

    def guarded(step, body):
        if has[step] is None:
            body()
        else:
            pl.when(has[step])(body)

    barrier = pltpu.get_barrier_semaphore()
    for step in (0, -1, 1):
        offsets = range(1, n_lon) if step == 0 else near

        def greet(step=step, offsets=offsets):
            for offset in offsets:
                pl.semaphore_signal(
                    barrier,
                    inc=1,
                    device_id=(lat + step, lax.rem(lon + offset, n_lon)),
                    device_id_type=MESH,
                )

        guarded(step, greet)
    sides = jnp.minimum(lat, 1) + jnp.minimum(n_lat - 1 - lat, 1)
    pl.semaphore_wait(barrier, n_lon - 1 + len(near) * sides)

    def field_copy(d, b):
        return pltpu.make_async_remote_copy(
            src_ref=fields.at[b],
            dst_ref=peers.at[d - 1, b],
            send_sem=f_send.at[d - 1, b],
            recv_sem=f_recv.at[d - 1, b],
            device_id=(lat, lax.rem(lon + d, n_lon)),
            device_id_type=MESH,
        )

    for b in range(batch):
        for d in range(1, n_lon):
            field_copy(d, b).start()

    def normalize(block):
        values = block.astype(F32)
        centred = values - jnp.mean(values, axis=-1, keepdims=True)
        variance = jnp.mean(centred * centred, axis=-1, keepdims=True)
        return (centred * lax.rsqrt(variance + 1e-05) * gain[...]).astype(BF16)

    w_t[0] = w_qkv[:, :width].T
    w_t[1] = w_qkv[:, 2 * width :].T

    for step, slot in ((-1, 0), (1, 2)):

        @pl.when(jnp.logical_not(has[step]))
        def _(slot=slot):
            hid[slot] = jnp.zeros_like(hid[slot])

    def attend(b, normed, first):
        keys = dot(normed, w_qkv[:, width : 2 * width]).astype(BF16)
        values_t = dot_nt(w_t[1], normed).astype(BF16)
        ones = jnp.ones((16, cols), BF16)
        for h in range(HEADS):
            rows = slice(h * depth, (h + 1) * depth)
            scores = dot(keys[:, rows], queries[b, rows, :])
            top = jnp.max(scores, axis=0, keepdims=True)
            if not first:
                old = maxima[b, h, 0:1, :]
                top = jnp.maximum(top, old)
                factor = jnp.exp2((old - top) * scale)
            maxima[b, h, 0:1, :] = top
            probs = jnp.exp2((scores - top) * scale).astype(BF16)
            summed = dot(jnp.concatenate([values_t[rows], ones], axis=0), probs)
            if first:
                acc[b, h] = summed
            else:
                acc[b, h] = acc[b, h] * factor + summed

    def local_block(b, carry):
        normed = normalize(fields[b])
        queries[b] = dot_nt(w_t[0], normed).astype(BF16)
        attend(b, normed, True)
        return carry

    lax.fori_loop(0, batch, local_block, 0)

    core = slice(EDGE, EDGE + cols)

    def halo(step, part, b):
        if part == 0:
            source, target, column = core, core, lon
        elif part == 1:
            source, target, column = slice(cols, EDGE + cols), slice(0, EDGE), right
        else:
            source, target, column = (
                slice(EDGE, 2 * EDGE),
                slice(EDGE + cols, 2 * EDGE + cols),
                left,
            )
        index = (step + 1) * 3 + part
        return pltpu.make_async_remote_copy(
            src_ref=hid.at[1, b, source],
            dst_ref=hid.at[1 - step, b, target],
            send_sem=h_send.at[b, index],
            recv_sem=h_recv.at[b, index],
            device_id=(lat + step, column),
            device_id_type=MESH,
        )

    parts = {-1: (0, 1, 2), 0: (1, 2), 1: (0, 1, 2)}

    def finish(b):
        for h in range(HEADS):
            att[h * depth : (h + 1) * depth, :] = (
                acc[b, h, :depth, :] / acc[b, h, depth : depth + 1, :]
            ).astype(BF16)
        update = dot(att[...].T, w_out[...])
        hid[1, b, core] = (fields[b].astype(F32) + update).astype(BF16)
        for step in (-1, 1, 0):

            def send(step=step):
                for part in parts[step]:
                    halo(step, part, b).start()

            guarded(step, send)

    for d in range(1, n_lon):

        def remote_block(b, carry, d=d):
            field_copy(d, b).wait_recv()
            attend(b, normalize(peers[d - 1, b]), False)
            if d == n_lon - 1:
                finish(b)
            return carry

        lax.fori_loop(0, batch, remote_block, 0)

    def upsample(b, carry):
        for step in (0, -1, 1):

            def arrive(step=step):
                for part in parts[step]:
                    halo(step, part, b).wait_recv()

            guarded(-step, arrive)
        for p in range(2):
            own, other = 1 + p, 3 * (1 - p)
            taps = dot(hid[1, b], conv_w[:, own * 4 * outward : (own + 1) * 4 * outward])
            taps = taps + dot(
                hid[2 * p, b], conv_w[:, other * 4 * outward : (other + 1) * 4 * outward]
            )
            even = (
                taps[EDGE : EDGE + cols, outward : 2 * outward]
                + taps[EDGE - 1 : EDGE - 1 + cols, 3 * outward :]
            )
            odd = (
                taps[EDGE : EDGE + cols, 2 * outward : 3 * outward]
                + taps[EDGE + 1 : EDGE + 1 + cols, :outward]
            )
            wide[pl.ds(0, cols, stride=2), :] = even + bias[...]
            wide[pl.ds(1, cols, stride=2), :] = odd + bias[...]
            out[b, p] = wide[...].astype(BF16)
        return carry

    lax.fori_loop(0, batch, upsample, 0)

    for b in range(batch):
        for d in range(1, n_lon):
            field_copy(d, b).wait_send()
        for step in (-1, 0, 1):

            def sent(step=step, b=b):
                for part in parts[step]:
                    halo(step, part, b).wait_send()

            guarded(step, sent)


def per_device(n_lat, n_lon, fields, norm_gain, w_qkv, w_out, conv_weight, conv_bias):
    batch, rows, cols, width = fields.shape
    assert rows == 1
    outward = conv_weight.shape[-1]
    depth = width // HEADS
    vmem = pl.BlockSpec(memory_space=pltpu.VMEM)
    return pl.pallas_call(
        functools.partial(kernel, n_lat, n_lon),
        out_shape=jax.ShapeDtypeStruct((batch, 2, 2 * cols, outward), BF16),
        in_specs=[vmem] * 6,
        out_specs=vmem,
        scratch_shapes=[
            pltpu.VMEM((n_lon - 1, batch, cols, width), BF16),
            pltpu.VMEM((batch, width, cols), BF16),
            pltpu.VMEM((2, width, width), BF16),
            pltpu.VMEM((batch, HEADS, depth + 16, cols), F32),
            pltpu.VMEM((batch, HEADS, 8, cols), F32),
            pltpu.VMEM((width, cols), BF16),
            pltpu.VMEM((3, batch, cols + 2 * EDGE, width), BF16),
            pltpu.VMEM((2 * cols, outward), F32),
            pltpu.SemaphoreType.DMA((n_lon - 1, batch)),
            pltpu.SemaphoreType.DMA((n_lon - 1, batch)),
            pltpu.SemaphoreType.DMA((batch, 9)),
            pltpu.SemaphoreType.DMA((batch, 9)),
        ],
        compiler_params=pltpu.CompilerParams(
            collective_id=0, has_side_effects=True, vmem_limit_bytes=48 * 1024 * 1024
        ),
        name="axial",
    )(
        fields.reshape(batch, cols, width),
        norm_gain.reshape(1, width),
        w_qkv,
        w_out,
        conv_weight.reshape(width, 16 * outward),
        conv_bias.reshape(1, outward),
    )


def solution(mesh):
    in_specs = (P(None, "lat", "lon", None), P(), P(), P(), P(), P())
    out_specs = P(None, "lat", "lon", None)
    return jax.shard_map(
        functools.partial(per_device, mesh.shape["lat"], mesh.shape["lon"]),
        mesh=mesh,
        in_specs=in_specs,
        out_specs=out_specs,
        check_vma=False,
    )
```

```python
import functools
import math

import jax
import jax.numpy as jnp
from jax import lax
from jax.experimental import pallas as pl
from jax.experimental.pallas import tpu as pltpu
from jax.sharding import PartitionSpec as P

HEADS = 8
EDGE = 16
GROUP = 128
CHUNKS = 2
MESH = pl.DeviceIdType.MESH
F32 = jnp.float32
BF16 = jnp.bfloat16


def dot(a, b):
    return jnp.dot(a, b, preferred_element_type=F32)


def dot_nt(a, b):
    return lax.dot_general(a, b, (((1,), (1,)), ((), ())), preferred_element_type=F32)


def kernel(
    n_lat,
    n_lon,
    fields,
    gain,
    w_qkv,
    w_out,
    conv_w,
    bias,
    out,
    peers,
    queries,
    acc,
    totals,
    maxima,
    hid,
    wide,
    f_send,
    f_recv,
    h_send,
    h_recv,
):
    batch, cols, width = fields.shape
    depth = width // HEADS
    chunk = cols // CHUNKS
    outward = bias.shape[-1]
    lat = lax.axis_index("lat")
    lon = lax.axis_index("lon")
    scale = depth ** (-0.5) * math.log2(math.e)
    right = lax.rem(lon + 1, n_lon)
    left = lax.rem(lon + n_lon - 1, n_lon)
    has = {-1: lat > 0, 0: None, 1: lat < n_lat - 1}
    near = sorted({0, 1, n_lon - 1})

    def guarded(step, body):
        if has[step] is None:
            body()
        else:
            pl.when(has[step])(body)

    barrier = pltpu.get_barrier_semaphore()
    for step in (0, -1, 1):
        offsets = range(1, n_lon) if step == 0 else near

        def greet(step=step, offsets=offsets):
            for offset in offsets:
                pl.semaphore_signal(
                    barrier,
                    inc=1,
                    device_id=(lat + step, lax.rem(lon + offset, n_lon)),
                    device_id_type=MESH,
                )

        guarded(step, greet)
    sides = jnp.minimum(lat, 1) + jnp.minimum(n_lat - 1 - lat, 1)
    pl.semaphore_wait(barrier, n_lon - 1 + len(near) * sides)

    def field_copy(d, b):
        return pltpu.make_async_remote_copy(
            src_ref=fields.at[b],
            dst_ref=peers.at[d - 1, b],
            send_sem=f_send.at[d - 1, b],
            recv_sem=f_recv.at[d - 1, b],
            device_id=(lat, lax.rem(lon + d, n_lon)),
            device_id_type=MESH,
        )

    for b in range(batch):
        for d in range(1, n_lon):
            field_copy(d, b).start()

    def normalize(block):
        values = block.astype(F32)
        centred = values - jnp.mean(values, axis=-1, keepdims=True)
        variance = jnp.mean(centred * centred, axis=-1, keepdims=True)
        return (centred * lax.rsqrt(variance + 1e-05) * gain[...]).astype(BF16)

    for step, slot in ((-1, 0), (1, 2)):

        @pl.when(jnp.logical_not(has[step]))
        def _(slot=slot):
            hid[slot] = jnp.zeros_like(hid[slot])

    head = lax.broadcasted_iota(jnp.int32, (chunk, GROUP), 1) // depth
    per_group = GROUP // depth

    def project(b, block, with_queries):
        normed = normalize(block)
        if with_queries:
            queries[b] = dot(normed, w_qkv[:, :width]).astype(BF16)
        keys = dot(normed, w_qkv[:, width : 2 * width]).astype(BF16)
        return keys, dot(normed, w_qkv[:, 2 * width :]).astype(BF16)

    def attend(b, c, keys, values, first):
        rows = slice(c * chunk, (c + 1) * chunk)
        for g in range(width // GROUP):
            lanes = slice(g * GROUP, (g + 1) * GROUP)
            query = queries[b, rows, lanes]
            stacked = jnp.concatenate(
                [query * (head == h).astype(BF16) for h in range(per_group)], axis=0
            )
            scores = dot_nt(stacked, keys[:, lanes])
            top = jnp.max(scores, axis=-1, keepdims=True)
            probs = jnp.exp2((scores - top) * scale).astype(BF16)
            ones = jnp.ones((cols, GROUP), BF16)
            mixed = dot(probs, jnp.concatenate([values[:, lanes], ones], axis=1))

            def merge(stack):
                merged = jnp.broadcast_to(stack[:chunk], (chunk, GROUP))
                for h in range(1, per_group):
                    merged = jnp.where(head == h, stack[h * chunk : (h + 1) * chunk], merged)
                return merged

            new_sum, new_total, new_top = (
                merge(mixed[:, :GROUP]),
                merge(mixed[:, GROUP:]),
                merge(top),
            )
            if not first:
                old_top = maxima[b, rows, lanes]
                both = jnp.maximum(old_top, new_top)
                old_factor = jnp.exp2((old_top - both) * scale)
                new_factor = jnp.exp2((new_top - both) * scale)
                new_sum = acc[b, rows, lanes] * old_factor + new_sum * new_factor
                new_total = totals[b, rows, lanes] * old_factor + new_total * new_factor
                new_top = both
            acc[b, rows, lanes] = new_sum
            totals[b, rows, lanes] = new_total
            maxima[b, rows, lanes] = new_top

    def local_block(b, carry):
        keys, values = project(b, fields[b], True)
        for c in range(CHUNKS):
            attend(b, c, keys, values, True)
        return carry

    lax.fori_loop(0, batch, local_block, 0)

    def halo(step, part, b):
        if part < CHUNKS:
            source = target = slice(EDGE + part * chunk, EDGE + (part + 1) * chunk)
            column = lon
        elif part == CHUNKS:
            source, target = slice(EDGE, 2 * EDGE), slice(EDGE + cols, 2 * EDGE + cols)
            column = left
        else:
            source, target, column = slice(cols, EDGE + cols), slice(0, EDGE), right
        index = (step + 1) * (CHUNKS + 2) + part
        return pltpu.make_async_remote_copy(
            src_ref=hid.at[1, b, source],
            dst_ref=hid.at[1 - step, b, target],
            send_sem=h_send.at[b, index],
            recv_sem=h_recv.at[b, index],
            device_id=(lat + step, column),
            device_id_type=MESH,
        )

    edges = (CHUNKS, CHUNKS + 1)
    parts = {-1: (*range(CHUNKS), *edges), 0: edges, 1: (*range(CHUNKS), *edges)}

    def finish(b, c):
        rows = slice(c * chunk, (c + 1) * chunk)
        attended = (acc[b, rows] / totals[b, rows]).astype(BF16)
        update = dot(attended, w_out[...])
        hid[1, b, EDGE + c * chunk : EDGE + (c + 1) * chunk] = (
            fields[b, rows].astype(F32) + update
        ).astype(BF16)
        ready = [c]
        if c == 0:
            ready.append(CHUNKS)
        if c == CHUNKS - 1:
            ready.append(CHUNKS + 1)
        for step in (-1, 1, 0):

            def send(step=step):
                for part in ready:
                    if part in parts[step]:
                        halo(step, part, b).start()

            guarded(step, send)

    for d in range(1, n_lon):

        def remote_block(b, carry, d=d):
            field_copy(d, b).wait_recv()
            keys, values = project(b, peers[d - 1, b], False)
            for c in range(CHUNKS):
                attend(b, c, keys, values, False)
                if d == n_lon - 1:
                    finish(b, c)
            return carry

        lax.fori_loop(0, batch, remote_block, 0)

    def upsample(b, carry):
        for step in (0, -1, 1):

            def arrive(step=step):
                for part in parts[step]:
                    halo(step, part, b).wait_recv()

            guarded(-step, arrive)
        for p in range(2):
            own, other = 1 + p, 3 * (1 - p)
            taps = dot(hid[1, b], conv_w[:, own * 4 * outward : (own + 1) * 4 * outward])
            taps = taps + dot(
                hid[2 * p, b], conv_w[:, other * 4 * outward : (other + 1) * 4 * outward]
            )
            even = (
                taps[EDGE : EDGE + cols, outward : 2 * outward]
                + taps[EDGE - 1 : EDGE - 1 + cols, 3 * outward :]
            )
            odd = (
                taps[EDGE : EDGE + cols, 2 * outward : 3 * outward]
                + taps[EDGE + 1 : EDGE + 1 + cols, :outward]
            )
            wide[pl.ds(0, cols, stride=2), :] = even + bias[...]
            wide[pl.ds(1, cols, stride=2), :] = odd + bias[...]
            out[b, p] = wide[...].astype(BF16)
        return carry

    lax.fori_loop(0, batch, upsample, 0)

    for b in range(batch):
        for d in range(1, n_lon):
            field_copy(d, b).wait_send()
        for step in (-1, 0, 1):

            def sent(step=step, b=b):
                for part in parts[step]:
                    halo(step, part, b).wait_send()

            guarded(step, sent)


def per_device(n_lat, n_lon, fields, norm_gain, w_qkv, w_out, conv_weight, conv_bias):
    batch, rows, cols, width = fields.shape
    assert rows == 1
    outward = conv_weight.shape[-1]
    vmem = pl.BlockSpec(memory_space=pltpu.VMEM)
    return pl.pallas_call(
        functools.partial(kernel, n_lat, n_lon),
        out_shape=jax.ShapeDtypeStruct((batch, 2, 2 * cols, outward), BF16),
        in_specs=[vmem] * 6,
        out_specs=vmem,
        scratch_shapes=[
            pltpu.VMEM((n_lon - 1, batch, cols, width), BF16),
            pltpu.VMEM((batch, cols, width), BF16),
            pltpu.VMEM((batch, cols, width), F32),
            pltpu.VMEM((batch, cols, width), F32),
            pltpu.VMEM((batch, cols, width), F32),
            pltpu.VMEM((3, batch, cols + 2 * EDGE, width), BF16),
            pltpu.VMEM((2 * cols, outward), F32),
            pltpu.SemaphoreType.DMA((n_lon - 1, batch)),
            pltpu.SemaphoreType.DMA((n_lon - 1, batch)),
            pltpu.SemaphoreType.DMA((batch, 3 * (CHUNKS + 2))),
            pltpu.SemaphoreType.DMA((batch, 3 * (CHUNKS + 2))),
        ],
        compiler_params=pltpu.CompilerParams(
            collective_id=0, has_side_effects=True, vmem_limit_bytes=48 * 1024 * 1024
        ),
        name="axial",
    )(
        fields.reshape(batch, cols, width),
        norm_gain.reshape(1, width),
        w_qkv,
        w_out,
        conv_weight.reshape(width, 16 * outward),
        conv_bias.reshape(1, outward),
    )


def solution(mesh):
    in_specs = (P(None, "lat", "lon", None), P(), P(), P(), P(), P())
    out_specs = P(None, "lat", "lon", None)
    return jax.shard_map(
        functools.partial(per_device, mesh.shape["lat"], mesh.shape["lon"]),
        mesh=mesh,
        in_specs=in_specs,
        out_specs=out_specs,
        check_vma=False,
    )
```
